256 devices in a mesh: freq: 16 (over y_hi, x, core), recv: 16 (over y_lo, z).
Axes of the slice: x: 4, y: 4 (y_hi: 2, y_lo: 2; y = y_hi * 2 + y_lo), z: 8, core: 2. Of those that a mesh axis runs over, the one named last changes fastest.
Arguments:
- response: bfloat16 [2, 256, 512, 4096], P(None, 'freq', 'recv'), may hold values from -0.0625 to 0.0625
- focusing: float32 [2, 256, 16, 4096], P(None, 'freq', None, 'recv'), may hold values from -6 to 6
- window_onset: int32 [16, 512], P(None, ('recv', 'freq')), may hold values from 0 to 511
- window_end: int32 [16, 512], P(None, ('recv', 'freq')), may hold values from 128 to 1023, as said below
Outputs:
- windowed: float32 [16, 512, 1024], P(None, ('recv', 'freq'))
The draws below stay inside these ranges and needn't reach their ends.
Inputs may be any that keep to these rules, and one draw needn't show every extreme that they name: window_end - window_onset lies between 128 and 512 for every trace.
All inputs are finite; a program needn't handle non-finite values.
Results may differ from the reference program's by a relative error of at most 0.0029.
Values may be sent and summed in bfloat16 or wider, within the bound.
No kernel may reach another device: no remote copies, remote signals or barrier semaphores. Data moves between devices by JAX's collectives and lax.ppermute only.
A program may use at most 64 MiB of HBM per device.

```python
import math
import jax
import jax.numpy as jnp
from jax import lax

NF = 256
NT = 1024
NS = 4096
F = 16
NR = 512


def window_pair(key):
    onset = jax.random.randint(jax.random.fold_in(key, 11), (F, NR), 0, NT // 2)
    length = jax.random.randint(jax.random.fold_in(key, 12), (F, NR), NT // 8, NT // 2 + 1)
    return (onset.astype(jnp.int32), (onset + length).astype(jnp.int32))


def draw_window_onset(key, part):
    return window_pair(key)[0]


def draw_window_end(key, part):
    return window_pair(key)[1]


def level_of(stream_key, dims, split, low, top_value):
    loudness, own = 1.0, jax.random.fold_in(stream_key, 6)
    for axis_at, blocks in split:
        draws = jnp.exp(jax.random.uniform(jax.random.fold_in(own, axis_at), (blocks,), jnp.float32, low / len(split), top_value / len(split)))
        loudness = loudness * jnp.repeat(draws, dims[axis_at] // blocks).reshape([-1 if axis == axis_at else 1 for axis in range(len(dims))])
    return loudness


def normal_values(stream_key, shape, spread, bound, pieces=(), kind=jnp.bfloat16):
    factor_of = level_of(stream_key, shape, pieces, -0.22, 0.18) if pieces else 1.0
    array = jax.random.normal(stream_key, shape, jnp.float32) * spread * factor_of
    return jnp.minimum(jnp.maximum(array, -bound), bound).astype(kind)


def setup_inputs(seed: int = 0) -> dict:
    keys = jax.random.split(jax.random.key(seed), 5)
    response = normal_values(keys[0], (2, NF, NR, NS), (2 * NS) ** -0.5, 0.0625, ((1, 16), (2, 16)))
    focusing = normal_values(keys[1], (2, NF, F, NS), 1.0, 6.0, ((1, 16), (3, 16)), jnp.float32)
    window_onset = draw_window_onset(jax.random.fold_in(keys[4], 71), 0)
    window_end = draw_window_end(jax.random.fold_in(keys[4], 71), 0)
    return {"response": response, "focusing": focusing, "window_onset": window_onset, "window_end": window_end}


def make_table(base, count):
    freqs = base + jnp.arange(count, dtype=jnp.int32)
    samples = jnp.arange(NT, dtype=jnp.int32)
    phase = (freqs[:, None] * samples[None, :] % NT).astype(jnp.float32) * (2.0 * math.pi / NT)
    scale = 1.0 / math.sqrt(NF)
    return jnp.stack([jnp.cos(phase) * scale, -jnp.sin(phase) * scale])

def reference(response, focusing, window_onset, window_end):
    focus_half = focusing.astype(jnp.bfloat16)

    def one_freq(index):
        real_resp = response[0, index]
        imag_resp = response[1, index]
        real_focus = focus_half[0, index]
        imag_focus = focus_half[1, index]
        real_part = jnp.dot(real_resp, real_focus.T, preferred_element_type=jnp.float32) - jnp.dot(imag_resp, imag_focus.T, preferred_element_type=jnp.float32)
        imag_part = jnp.dot(real_resp, imag_focus.T, preferred_element_type=jnp.float32) + jnp.dot(imag_resp, real_focus.T, preferred_element_type=jnp.float32)
        return jnp.stack([real_part, imag_part])
    spectra = lax.map(one_freq, jnp.arange(NF, dtype=jnp.int32))
    table = make_table(0, NF)
    traces = jnp.einsum('kcrq,ckt->qrt', spectra, table, precision=lax.Precision.HIGHEST)
    samples = jnp.arange(NT, dtype=jnp.int32)
    keep = (samples[None, None, :] >= window_onset[:, :, None]) & (samples[None, None, :] < window_end[:, :, None])
    return jnp.where(keep, traces, jnp.float32(0.0))
```

```python
import math

import jax
import jax.numpy as jnp
import ml_dtypes
import numpy as np
from jax import lax
from jax.experimental import pallas as pl
from jax.experimental.pallas import tpu as pltpu
from jax.sharding import PartitionSpec as P

NF = 256
NT = 1024
Z = 8

UP = [(y * Z + z, y * Z + (z + 1) % Z) for y in range(2) for z in range(Z)]
DOWN = [(b, a) for a, b in UP]
ACROSS = [(i, (i + Z) % (2 * Z)) for i in range(2 * Z)]

STEPS = [
    [((0, -1), (0, 0), UP), ((0, 1), (0, 0), DOWN), ((1, 0), (0, 0), ACROSS)],
    [((0, -2), (0, -1), UP), ((0, 2), (0, 1), DOWN), ((1, -1), (0, -1), ACROSS)],
    [((0, -3), (0, -2), UP), ((0, 3), (0, 2), DOWN), ((1, 1), (0, 1), ACROSS)],
    [((0, -4), (0, -3), UP), ((1, 2), (1, 1), DOWN), ((1, -2), (0, -2), ACROSS)],
    [((1, -3), (1, -2), UP), ((1, 3), (1, 2), DOWN), ((1, -4), (0, -4), ACROSS)],
]
ORDER = [(0, 0)] + [key for step in STEPS for key, _, _ in step]

KC = 8


def make_table():
    phase = (np.arange(NF)[:, None] * np.arange(NT)[None, :] % NT) * (2.0 * np.pi / NT)
    scale = 1.0 / math.sqrt(NF)
    table = np.concatenate([np.cos(phase) * scale, -np.sin(phase) * scale], 0)
    table = table.reshape(2, NF // 16, 2, KC, NT).transpose(2, 0, 1, 3, 4).reshape(2 * NF, NT)
    high = table.astype(ml_dtypes.bfloat16)
    low = (table - high.astype(np.float64)).astype(ml_dtypes.bfloat16)
    return high, low


def contract_kernel(count, first, last, place_ref, *refs):
    responses, blocks, rest = refs[:count], refs[count : 2 * count], refs[2 * count :]
    out_ref = rest[-1] if not last else rest[-2]
    dims = (((1,), (1,)), ((), ()))
    for k in range(KC):
        total = None if first else rest[0][k]
        for response, block in zip(responses, blocks):
            real, imag = block[0, k], block[1, k]
            for part, right in (
                (response[0, k], jnp.concatenate([real, imag], 0)),
                (response[1, k], jnp.concatenate([-imag, real], 0)),
            ):
                term = lax.dot_general(part, right, dims, preferred_element_type=jnp.float32)
                total = term if total is None else total + term
        if not last:
            out_ref[k] = total
        else:
            rest[-1][k] = total
    if last:
        totals = rest[-1]
        width = totals.shape[2]
        for half in range(out_ref.shape[2] // (2 * width)):

            @pl.when(pl.program_id(0) == half)
            def _():
                for k in range(KC):
                    for parity in range(2):
                        lane = (2 * half + parity) * width
                        out_ref[:, k, lane : lane + width] = totals[k, pl.ds(parity, out_ref.shape[0], stride=2), :]


def contract(response, place, keys, blocks, total, last):
    freqs, recvs, focal = response.shape[1], response.shape[2], blocks[0].shape[2]
    width = blocks[0].shape[3]
    count, first = len(blocks), total is None

    def source(g, at, key):
        column, offset = key
        return 0, g, 0, ((at[0] & Z) ^ (Z * column)) | ((at[0] + (offset % Z)) & (Z - 1))

    in_specs = [
        pl.BlockSpec((2, KC, recvs, width), lambda g, at, key=key: source(g, at, key)) for key in keys
    ] + [pl.BlockSpec((2, KC, focal, width), lambda g, at: (0, g, 0, 0))] * count
    acc_spec = pl.BlockSpec((KC, recvs, 2 * focal), lambda g, at: (g, 0, 0))
    args = [response] * count + list(blocks)
    if not first:
        in_specs.append(acc_spec)
        args.append(total)
    if last:
        shape = (recvs // 2, KC, freqs // KC * 4 * focal)
        out_spec = pl.BlockSpec(shape, lambda g, at: (0, 0, 0))
        scratch = [pltpu.VMEM((KC, recvs, 2 * focal), jnp.float32)]
    else:
        shape = (freqs, recvs, 2 * focal)
        out_spec, scratch = acc_spec, []
    return pl.pallas_call(
        lambda *refs: contract_kernel(count, first, last, *refs),
        out_shape=jax.ShapeDtypeStruct(shape, jnp.float32),
        grid_spec=pltpu.PrefetchScalarGridSpec(
            num_scalar_prefetch=1,
            grid=(freqs // KC,),
            in_specs=in_specs,
            out_specs=out_spec,
            scratch_shapes=scratch,
        ),
        compiler_params=pltpu.CompilerParams(vmem_limit_bytes=16 * 2**20),
        cost_estimate=pl.CostEstimate(
            flops=count * freqs * recvs * focal * width * 8,
            bytes_accessed=count * freqs * (recvs + focal) * width * 4,
            transcendentals=0,
        ),
        name="contract",
    )(place, *args)


def split(x):
    high = x.astype(jnp.bfloat16)
    return high, (x - high.astype(jnp.float32)).astype(jnp.bfloat16)


def transform_kernel(moved_ref, high_ref, low_ref, start_ref, end_ref, out_ref):
    across = moved_ref[...].T
    rows = jnp.concatenate(
        [
            jnp.concatenate(
                [across[64 * half + 32 * parity + 16 * part :][:16] for half in range(2) for part in range(2)], 1
            )
            for parity in range(2)
        ],
        0,
    )
    high, low = split(rows)
    both = jnp.concatenate([high, low], 0)
    dims = (((1,), (0,)), ((), ()))
    width = 256
    for at in range(0, NT, width):
        cols = slice(at, at + width)
        main = lax.dot_general(both, high_ref[:, cols], dims, preferred_element_type=jnp.float32)
        rest = lax.dot_general(high, low_ref[:, cols], dims, preferred_element_type=jnp.float32)
        traces = main[0:32] + (main[32:64] + rest)
        samples = lax.broadcasted_iota(jnp.int32, traces.shape, 1) + at
        keep = (samples >= start_ref[...]) & (samples < end_ref[...])
        traces = jnp.where(keep, traces, 0.0)
        for parity in range(2):
            out_ref[:, parity, cols] = traces[16 * parity : 16 * parity + 16]


def transform(moved, high, low, start, end, focal):
    return pl.pallas_call(
        transform_kernel,
        out_shape=jax.ShapeDtypeStruct((focal, 2, NT), jnp.float32),
        compiler_params=pltpu.CompilerParams(vmem_limit_bytes=16 * 2**20),
        cost_estimate=pl.CostEstimate(flops=32 * 512 * NT * 6, bytes_accessed=2**21, transcendentals=0),
        name="transform",
    )(moved, high, low, start, end)


def per_device(response, focusing, window_onset, window_end):
    focal = focusing.shape[2]
    place = lax.axis_index("recv").astype(jnp.int32).reshape(1)
    blocks = {(0, 0): focusing.astype(jnp.bfloat16)}
    for step in STEPS:
        for key, source, perm in step:
            blocks[key] = lax.ppermute(blocks[source], "recv", perm)
    total = None
    for keys in [ORDER[:1]] + [ORDER[at : at + 3] for at in range(1, 16, 3)]:
        total = contract(response, place, keys, [blocks[key] for key in keys], total, ORDER[-1] in keys)
    moved = lax.all_to_all(total, "freq", split_axis=0, concat_axis=0, tiled=True)
    moved = moved.reshape(-1, moved.shape[2])
    high, low = make_table()
    start = window_onset.T.reshape(2 * focal, 1)
    end = window_end.T.reshape(2 * focal, 1)
    return transform(moved, jnp.asarray(high), jnp.asarray(low), start, end, focal)


def solution(mesh):
    in_specs = (
        P(None, "freq", "recv", None),
        P(None, "freq", None, "recv"),
        P(None, ("recv", "freq")),
        P(None, ("recv", "freq")),
    )
    out_specs = P(None, ("recv", "freq"), None)
    return jax.shard_map(
        per_device, mesh=mesh, in_specs=in_specs, out_specs=out_specs, check_vma=False
    )
```

```python
import math

import jax
import jax.numpy as jnp
import ml_dtypes
import numpy as np
from jax import lax
from jax.experimental import pallas as pl
from jax.experimental.pallas import tpu as pltpu
from jax.sharding import PartitionSpec as P

NF = 256
NT = 1024
Z = 8

UP = [(y * Z + z, y * Z + (z + 1) % Z) for y in range(2) for z in range(Z)]
DOWN = [(b, a) for a, b in UP]
ACROSS = [(i, (i + Z) % (2 * Z)) for i in range(2 * Z)]

STEPS = [
    [((0, -1), (0, 0), UP), ((0, 1), (0, 0), DOWN), ((1, 0), (0, 0), ACROSS)],
    [((0, -2), (0, -1), UP), ((0, 2), (0, 1), DOWN), ((1, 1), (0, 1), ACROSS)],
    [((0, -3), (0, -2), UP), ((0, 3), (0, 2), DOWN), ((1, -2), (0, -2), ACROSS)],
    [((0, -4), (0, -3), UP), ((1, 2), (1, 1), DOWN), ((1, -1), (0, -1), ACROSS)],
    [((1, -3), (1, -2), UP), ((1, 3), (1, 2), DOWN), ((1, -4), (0, -4), ACROSS)],
]
LAST = [[send[0] for send in STEPS[3]], [send[0] for send in STEPS[4][:2]], [STEPS[4][2][0]]]
SENDS = [send for step in STEPS for send in step]

COST = 0.1e9
KC = 8


def make_table():
    phase = (np.arange(NF)[:, None] * np.arange(NT)[None, :] % NT) * (2.0 * np.pi / NT)
    scale = 1.0 / math.sqrt(NF)
    table = np.concatenate([np.cos(phase) * scale, -np.sin(phase) * scale], 0)
    table = table.reshape(2, NF // 16, 2, KC, NT).transpose(2, 0, 1, 3, 4).reshape(2 * NF, NT)
    high = table.astype(ml_dtypes.bfloat16)
    low = (table - high.astype(np.float64)).astype(ml_dtypes.bfloat16)
    return high, low


def contract_kernel(count, first, last, place_ref, *refs):
    responses, blocks, rest = refs[:count], refs[count : 2 * count], refs[2 * count :]
    out_ref = rest[-1] if not last else rest[-2]
    dims = (((1,), (1,)), ((), ()))
    for k in range(KC):
        total = None if first else rest[0][k]
        for response, block in zip(responses, blocks):
            real, imag = block[0, k], block[1, k]
            for part, right in (
                (response[0, k], jnp.concatenate([real, imag], 0)),
                (response[1, k], jnp.concatenate([-imag, real], 0)),
            ):
                term = lax.dot_general(part, right, dims, preferred_element_type=jnp.float32)
                total = term if total is None else total + term
        if not last:
            out_ref[k] = total
        else:
            rest[-1][k] = total
    if last:
        totals = rest[-1]
        width = totals.shape[2]
        for half in range(out_ref.shape[2] // (2 * width)):

            @pl.when(pl.program_id(0) == half)
            def _():
                for k in range(KC):
                    for parity in range(2):
                        lane = (2 * half + parity) * width
                        out_ref[:, k, lane : lane + width] = totals[k, pl.ds(parity, out_ref.shape[0], stride=2), :]


def contract(response, place, keys, blocks, total, last):
    freqs, recvs, focal = response.shape[1], response.shape[2], blocks[0].shape[2]
    width = blocks[0].shape[3]
    count, first = len(blocks), total is None

    def source(g, at, key):
        column, distance = key
        return 0, g, 0, ((at[0] & Z) ^ (Z * column)) | ((at[0] + distance) & (Z - 1))

    in_specs = [
        pl.BlockSpec((2, KC, recvs, width), lambda g, at, key=key: source(g, at, key)) for key in keys
    ] + [pl.BlockSpec((2, KC, focal, width), lambda g, at: (0, g, 0, 0))] * count
    acc_spec = pl.BlockSpec((KC, recvs, 2 * focal), lambda g, at: (g, 0, 0))
    args = [response] * count + list(blocks)
    if not first:
        in_specs.append(acc_spec)
        args.append(total)
    if last:
        shape = (recvs // 2, KC, freqs // KC * 4 * focal)
        out_spec = pl.BlockSpec(shape, lambda g, at: (0, 0, 0))
        scratch = [pltpu.VMEM((KC, recvs, 2 * focal), jnp.float32)]
    else:
        shape = (freqs, recvs, 2 * focal)
        out_spec, scratch = acc_spec, []
    return pl.pallas_call(
        lambda *refs: contract_kernel(count, first, last, *refs),
        out_shape=jax.ShapeDtypeStruct(shape, jnp.float32),
        grid_spec=pltpu.PrefetchScalarGridSpec(
            num_scalar_prefetch=1,
            grid=(freqs // KC,),
            in_specs=in_specs,
            out_specs=out_spec,
            scratch_shapes=scratch,
        ),
        compiler_params=pltpu.CompilerParams(vmem_limit_bytes=16 * 2**20),
        cost_estimate=pl.CostEstimate(
            flops=int(COST * count),
            bytes_accessed=count * freqs * (recvs + focal) * width * 4,
            transcendentals=0,
        ),
        name="contract",
    )(place, *args)


def split(x):
    high = x.astype(jnp.bfloat16)
    return high, (x - high.astype(jnp.float32)).astype(jnp.bfloat16)


def transform_kernel(moved_ref, high_ref, low_ref, start_ref, end_ref, out_ref):
    across = moved_ref[...].T
    rows = jnp.concatenate(
        [
            jnp.concatenate(
                [across[64 * half + 32 * parity + 16 * part :][:16] for half in range(2) for part in range(2)], 1
            )
            for parity in range(2)
        ],
        0,
    )
    high, low = split(rows)
    both = jnp.concatenate([high, low], 0)
    dims = (((1,), (0,)), ((), ()))
    width = 256
    for at in range(0, NT, width):
        cols = slice(at, at + width)
        main = lax.dot_general(both, high_ref[:, cols], dims, preferred_element_type=jnp.float32)
        rest = lax.dot_general(high, low_ref[:, cols], dims, preferred_element_type=jnp.float32)
        traces = main[0:32] + (main[32:64] + rest)
        samples = lax.broadcasted_iota(jnp.int32, traces.shape, 1) + at
        keep = (samples >= start_ref[...]) & (samples < end_ref[...])
        traces = jnp.where(keep, traces, 0.0)
        for parity in range(2):
            out_ref[:, parity, cols] = traces[16 * parity : 16 * parity + 16]


def transform(moved, high, low, start, end, focal):
    return pl.pallas_call(
        transform_kernel,
        out_shape=jax.ShapeDtypeStruct((focal, 2, NT), jnp.float32),
        compiler_params=pltpu.CompilerParams(vmem_limit_bytes=16 * 2**20),
        cost_estimate=pl.CostEstimate(flops=32 * 512 * NT * 6, bytes_accessed=2**21, transcendentals=0),
        name="transform",
    )(moved, high, low, start, end)


def per_device(response, focusing, window_onset, window_end):
    focal = focusing.shape[2]
    place = lax.axis_index("recv").astype(jnp.int32).reshape(1)
    blocks = {(0, 0): focusing.astype(jnp.bfloat16)}
    total = contract(response, place, [(0, 0)], [blocks[(0, 0)]], None, False)
    for at, (key, source, perm) in enumerate(SENDS):
        value = blocks[source]
        before = SENDS[at - 3][0] if at >= 3 else source
        if at >= 3 and at % 3 == 0:
            value, total = lax.optimization_barrier((value, total))
        if before != source:
            value, blocks[before] = lax.optimization_barrier((value, blocks[before]))
        blocks[key] = lax.ppermute(value, "recv", perm)
        if 5 <= at < 14 and at % 3 == 2:
            keys = [send[0] for send in STEPS[at // 3 - 1]]
            total = contract(response, place, keys, [blocks[k] for k in keys], total, False)
    for keys in LAST:
        total = contract(response, place, keys, [blocks[k] for k in keys], total, keys is LAST[-1])
    moved = lax.all_to_all(total, "freq", split_axis=0, concat_axis=0, tiled=True)
    moved = moved.reshape(-1, moved.shape[2])
    high, low = make_table()
    start = window_onset.T.reshape(2 * focal, 1)
    end = window_end.T.reshape(2 * focal, 1)
    return transform(moved, jnp.asarray(high), jnp.asarray(low), start, end, focal)


def solution(mesh):
    in_specs = (
        P(None, "freq", "recv", None),
        P(None, "freq", None, "recv"),
        P(None, ("recv", "freq")),
        P(None, ("recv", "freq")),
    )
    out_specs = P(None, ("recv", "freq"), None)
    return jax.shard_map(
        per_device, mesh=mesh, in_specs=in_specs, out_specs=out_specs, check_vma=False
    )
```

```python
import math

import jax
import jax.numpy as jnp
import ml_dtypes
import numpy as np
from jax import lax
from jax.experimental import pallas as pl
from jax.experimental.pallas import tpu as pltpu
from jax.sharding import PartitionSpec as P

NF = 256
NT = 1024
Z = 8

UP = [(y * Z + z, y * Z + (z + 1) % Z) for y in range(2) for z in range(Z)]
DOWN = [(b, a) for a, b in UP]
ACROSS = [(i, (i + Z) % (2 * Z)) for i in range(2 * Z)]

STEPS = [
    [((0, -1), (0, 0), UP), ((0, 1), (0, 0), DOWN), ((1, 0), (0, 0), ACROSS)],
    [((0, -2), (0, -1), UP), ((0, 2), (0, 1), DOWN), ((1, 1), (0, 1), ACROSS)],
    [((0, -3), (0, -2), UP), ((0, 3), (0, 2), DOWN), ((1, -2), (0, -2), ACROSS)],
    [((0, -4), (0, -3), UP), ((1, 2), (1, 1), DOWN), ((1, -1), (0, -1), ACROSS)],
    [((1, -3), (1, -2), UP), ((1, 3), (1, 2), DOWN), ((1, -4), (0, -4), ACROSS)],
]
LAST = [[send[0] for send in STEPS[3]], [send[0] for send in STEPS[4][:2]], [STEPS[4][2][0]]]
SENDS = [send for step in STEPS for send in step]

COST = 0.1e9
KC = 8


def make_table():
    phase = (np.arange(NF)[:, None] * np.arange(NT)[None, :] % NT) * (2.0 * np.pi / NT)
    scale = 1.0 / math.sqrt(NF)
    table = np.concatenate([np.cos(phase) * scale, -np.sin(phase) * scale], 0)
    table = table.reshape(2, NF // 16, 2, KC, NT).transpose(2, 0, 1, 3, 4).reshape(2 * NF, NT)
    high = table.astype(ml_dtypes.bfloat16)
    low = (table - high.astype(np.float64)).astype(ml_dtypes.bfloat16)
    return high, low


def contract_kernel(count, chunk, first, last, place_ref, *refs):
    responses, blocks, rest = refs[:count], refs[count : 2 * count], refs[2 * count :]
    out_ref = rest[-1] if not last else rest[-2]
    dims = (((1,), (1,)), ((), ()))
    for k in range(chunk):
        total = None if first else rest[0][k]
        for response, block in zip(responses, blocks):
            real, imag = block[0, k], block[1, k]
            for part, right in (
                (response[0, k], jnp.concatenate([real, imag], 0)),
                (response[1, k], jnp.concatenate([-imag, real], 0)),
            ):
                term = lax.dot_general(part, right, dims, preferred_element_type=jnp.float32)
                total = term if total is None else total + term
        if not last:
            out_ref[k] = total
        else:
            rest[-1][k] = total
    if last:
        totals = rest[-1]
        width = totals.shape[2]
        for half in range(chunk // KC):
            for k in range(KC):
                for parity in range(2):
                    lane = (2 * half + parity) * width
                    rows = totals[half * KC + k, pl.ds(parity, out_ref.shape[0], stride=2), :]
                    out_ref[:, k, lane : lane + width] = rows


def contract(response, place, keys, blocks, total, last):
    freqs, recvs, focal = response.shape[1], response.shape[2], blocks[0].shape[2]
    width = blocks[0].shape[3]
    count, first = len(blocks), total is None
    chunk = freqs

    def source(g, at, key):
        column, distance = key
        return 0, g, 0, ((at[0] & Z) ^ (Z * column)) | ((at[0] + distance) & (Z - 1))

    in_specs = [
        pl.BlockSpec((2, chunk, recvs, width), lambda g, at, key=key: source(g, at, key)) for key in keys
    ] + [pl.BlockSpec((2, chunk, focal, width), lambda g, at: (0, g, 0, 0))] * count
    acc_spec = pl.BlockSpec((chunk, recvs, 2 * focal), lambda g, at: (g, 0, 0))
    args = [response] * count + list(blocks)
    if not first:
        in_specs.append(acc_spec)
        args.append(total)
    if last:
        shape = (recvs // 2, KC, freqs // KC * 4 * focal)
        out_spec = pl.BlockSpec(shape, lambda g, at: (0, 0, 0))
        scratch = [pltpu.VMEM((chunk, recvs, 2 * focal), jnp.float32)]
    else:
        shape = (freqs, recvs, 2 * focal)
        out_spec, scratch = acc_spec, []
    return pl.pallas_call(
        lambda *refs: contract_kernel(count, chunk, first, last, *refs),
        out_shape=jax.ShapeDtypeStruct(shape, jnp.float32),
        grid_spec=pltpu.PrefetchScalarGridSpec(
            num_scalar_prefetch=1,
            grid=(freqs // chunk,),
            in_specs=in_specs,
            out_specs=out_spec,
            scratch_shapes=scratch,
        ),
        compiler_params=pltpu.CompilerParams(vmem_limit_bytes=16 * 2**20),
        cost_estimate=pl.CostEstimate(
            flops=int(COST * count),
            bytes_accessed=count * freqs * (recvs + focal) * width * 4,
            transcendentals=0,
        ),
        name="contract",
    )(place, *args)


def split(x):
    high = x.astype(jnp.bfloat16)
    return high, (x - high.astype(jnp.float32)).astype(jnp.bfloat16)


def transform_kernel(moved_ref, high_ref, low_ref, start_ref, end_ref, out_ref):
    across = moved_ref[...].T
    rows = jnp.concatenate(
        [
            jnp.concatenate(
                [across[64 * half + 32 * parity + 16 * part :][:16] for half in range(2) for part in range(2)], 1
            )
            for parity in range(2)
        ],
        0,
    )
    high, low = split(rows)
    both = jnp.concatenate([high, low], 0)
    dims = (((1,), (0,)), ((), ()))
    width = 256
    for at in range(0, NT, width):
        cols = slice(at, at + width)
        main = lax.dot_general(both, high_ref[:, cols], dims, preferred_element_type=jnp.float32)
        rest = lax.dot_general(high, low_ref[:, cols], dims, preferred_element_type=jnp.float32)
        traces = main[0:32] + (main[32:64] + rest)
        samples = lax.broadcasted_iota(jnp.int32, traces.shape, 1) + at
        keep = (samples >= start_ref[...]) & (samples < end_ref[...])
        traces = jnp.where(keep, traces, 0.0)
        for parity in range(2):
            out_ref[:, parity, cols] = traces[16 * parity : 16 * parity + 16]


def transform(moved, high, low, start, end, focal):
    return pl.pallas_call(
        transform_kernel,
        out_shape=jax.ShapeDtypeStruct((focal, 2, NT), jnp.float32),
        compiler_params=pltpu.CompilerParams(vmem_limit_bytes=16 * 2**20),
        cost_estimate=pl.CostEstimate(flops=32 * 512 * NT * 6, bytes_accessed=2**21, transcendentals=0),
        name="transform",
    )(moved, high, low, start, end)


def per_device(response, focusing, window_onset, window_end):
    focal = focusing.shape[2]
    place = lax.axis_index("recv").astype(jnp.int32).reshape(1)
    blocks = {(0, 0): focusing.astype(jnp.bfloat16)}
    total = contract(response, place, [(0, 0)], [blocks[(0, 0)]], None, False)
    for at, (key, source, perm) in enumerate(SENDS):
        value = blocks[source]
        before = SENDS[at - 3][0] if at >= 3 else source
        if at >= 3 and at % 3 == 0:
            value, total = lax.optimization_barrier((value, total))
        if before != source:
            value, blocks[before] = lax.optimization_barrier((value, blocks[before]))
        blocks[key] = lax.ppermute(value, "recv", perm)
        if 5 <= at < 14 and at % 3 == 2:
            keys = [send[0] for send in STEPS[at // 3 - 1]]
            total = contract(response, place, keys, [blocks[k] for k in keys], total, False)
    for keys in LAST:
        total = contract(response, place, keys, [blocks[k] for k in keys], total, keys is LAST[-1])
    moved = lax.all_to_all(total, "freq", split_axis=0, concat_axis=0, tiled=True)
    moved = moved.reshape(-1, moved.shape[2])
    high, low = make_table()
    start = window_onset.T.reshape(2 * focal, 1)
    end = window_end.T.reshape(2 * focal, 1)
    return transform(moved, jnp.asarray(high), jnp.asarray(low), start, end, focal)


def solution(mesh):
    in_specs = (
        P(None, "freq", "recv", None),
        P(None, "freq", None, "recv"),
        P(None, ("recv", "freq")),
        P(None, ("recv", "freq")),
    )
    out_specs = P(None, ("recv", "freq"), None)
    return jax.shard_map(
        per_device, mesh=mesh, in_specs=in_specs, out_specs=out_specs, check_vma=False
    )
```

```python
import math

import jax
import jax.numpy as jnp
import ml_dtypes
import numpy as np
from jax import lax
from jax.experimental import pallas as pl
from jax.experimental.pallas import tpu as pltpu
from jax.sharding import PartitionSpec as P

NF = 256
NT = 1024
Z = 8

UP = [(y * Z + z, y * Z + (z + 1) % Z) for y in range(2) for z in range(Z)]
DOWN = [(b, a) for a, b in UP]
ACROSS = [(i, (i + Z) % (2 * Z)) for i in range(2 * Z)]

STEPS = [
    [((0, -1), (0, 0), UP), ((0, 1), (0, 0), DOWN), ((1, 0), (0, 0), ACROSS)],
    [((0, -2), (0, -1), UP), ((0, 2), (0, 1), DOWN), ((1, 1), (0, 1), ACROSS)],
    [((0, -3), (0, -2), UP), ((0, 3), (0, 2), DOWN), ((1, -2), (0, -2), ACROSS)],
    [((0, -4), (0, -3), UP), ((1, 2), (1, 1), DOWN), ((1, -1), (0, -1), ACROSS)],
    [((1, -3), (1, -2), UP), ((1, 3), (1, 2), DOWN), ((1, -4), (0, -4), ACROSS)],
]
LAST = [[send[0] for send in STEPS[3]], [send[0] for send in STEPS[4]]]
SENDS = [send for step in STEPS for send in step]

COST = 0.1e9
KC = 8


def make_table():
    phase = (np.arange(NF)[:, None] * np.arange(NT)[None, :] % NT) * (2.0 * np.pi / NT)
    scale = 1.0 / math.sqrt(NF)
    table = np.concatenate([np.cos(phase) * scale, -np.sin(phase) * scale], 0)
    table = table.reshape(2, NF // 16, 2, KC, NT).transpose(2, 0, 1, 3, 4).reshape(2 * NF, NT)
    high = table.astype(ml_dtypes.bfloat16)
    low = (table - high.astype(np.float64)).astype(ml_dtypes.bfloat16)
    return high, low


def contract_kernel(count, chunk, first, last, place_ref, *refs):
    responses, blocks, rest = refs[:count], refs[count : 2 * count], refs[2 * count :]
    out_ref = rest[-1] if not last else rest[-2]
    dims = (((1,), (1,)), ((), ()))
    for k in range(chunk):
        total = None if first else rest[0][k]
        for response, block in zip(responses, blocks):
            real, imag = block[0, k], block[1, k]
            for part, right in (
                (response[0, k], jnp.concatenate([real, imag], 0)),
                (response[1, k], jnp.concatenate([-imag, real], 0)),
            ):
                term = lax.dot_general(part, right, dims, preferred_element_type=jnp.float32)
                total = term if total is None else total + term
        if not last:
            out_ref[k] = total
        else:
            rest[-1][k] = total
    if last:
        totals = rest[-1]
        width = totals.shape[2]
        for half in range(chunk // KC):
            for k in range(KC):
                for parity in range(2):
                    lane = (2 * half + parity) * width
                    rows = totals[half * KC + k, pl.ds(parity, out_ref.shape[0], stride=2), :]
                    out_ref[:, k, lane : lane + width] = rows


def contract(response, place, keys, blocks, total, last):
    freqs, recvs, focal = response.shape[1], response.shape[2], blocks[0].shape[2]
    width = blocks[0].shape[3]
    count, first = len(blocks), total is None
    chunk = freqs

    def source(g, at, key):
        column, distance = key
        return 0, g, 0, ((at[0] & Z) ^ (Z * column)) | ((at[0] + distance) & (Z - 1))

    in_specs = [
        pl.BlockSpec((2, chunk, recvs, width), lambda g, at, key=key: source(g, at, key)) for key in keys
    ] + [pl.BlockSpec((2, chunk, focal, width), lambda g, at: (0, g, 0, 0))] * count
    acc_spec = pl.BlockSpec((chunk, recvs, 2 * focal), lambda g, at: (g, 0, 0))
    args = [response] * count + list(blocks)
    if not first:
        in_specs.append(acc_spec)
        args.append(total)
    if last:
        shape = (recvs // 2, KC, freqs // KC * 4 * focal)
        out_spec = pl.BlockSpec(shape, lambda g, at: (0, 0, 0))
        scratch = [pltpu.VMEM((chunk, recvs, 2 * focal), jnp.float32)]
    else:
        shape = (freqs, recvs, 2 * focal)
        out_spec, scratch = acc_spec, []
    return pl.pallas_call(
        lambda *refs: contract_kernel(count, chunk, first, last, *refs),
        out_shape=jax.ShapeDtypeStruct(shape, jnp.float32),
        grid_spec=pltpu.PrefetchScalarGridSpec(
            num_scalar_prefetch=1,
            grid=(freqs // chunk,),
            in_specs=in_specs,
            out_specs=out_spec,
            scratch_shapes=scratch,
        ),
        compiler_params=pltpu.CompilerParams(vmem_limit_bytes=16 * 2**20),
        cost_estimate=pl.CostEstimate(
            flops=int(COST * count),
            bytes_accessed=count * freqs * (recvs + focal) * width * 4,
            transcendentals=0,
        ),
        name="contract",
    )(place, *args)


def split(x):
    high = x.astype(jnp.bfloat16)
    return high, (x - high.astype(jnp.float32)).astype(jnp.bfloat16)


def transform_kernel(moved_ref, high_ref, low_ref, start_ref, end_ref, out_ref):
    across = moved_ref[...].T
    rows = jnp.concatenate(
        [
            jnp.concatenate(
                [across[64 * half + 32 * parity + 16 * part :][:16] for half in range(2) for part in range(2)], 1
            )
            for parity in range(2)
        ],
        0,
    )
    high, low = split(rows)
    both = jnp.concatenate([high, low], 0)
    dims = (((1,), (0,)), ((), ()))
    width = 256
    for at in range(0, NT, width):
        cols = slice(at, at + width)
        main = lax.dot_general(both, high_ref[:, cols], dims, preferred_element_type=jnp.float32)
        rest = lax.dot_general(high, low_ref[:, cols], dims, preferred_element_type=jnp.float32)
        traces = main[0:32] + (main[32:64] + rest)
        samples = lax.broadcasted_iota(jnp.int32, traces.shape, 1) + at
        keep = (samples >= start_ref[...]) & (samples < end_ref[...])
        traces = jnp.where(keep, traces, 0.0)
        for parity in range(2):
            out_ref[:, parity, cols] = traces[16 * parity : 16 * parity + 16]


def transform(moved, high, low, start, end, focal):
    return pl.pallas_call(
        transform_kernel,
        out_shape=jax.ShapeDtypeStruct((focal, 2, NT), jnp.float32),
        compiler_params=pltpu.CompilerParams(vmem_limit_bytes=16 * 2**20),
        cost_estimate=pl.CostEstimate(flops=32 * 512 * NT * 6, bytes_accessed=2**21, transcendentals=0),
        name="transform",
    )(moved, high, low, start, end)


def per_device(response, focusing, window_onset, window_end):
    focal = focusing.shape[2]
    place = lax.axis_index("recv").astype(jnp.int32).reshape(1)
    blocks = {(0, 0): focusing.astype(jnp.bfloat16)}
    total = contract(response, place, [(0, 0)], [blocks[(0, 0)]], None, False)
    for at, (key, source, perm) in enumerate(SENDS):
        value = blocks[source]
        before = SENDS[at - 3][0] if at >= 3 else source
        if at >= 3 and at % 3 == 0:
            value, total = lax.optimization_barrier((value, total))
        if before != source:
            value, blocks[before] = lax.optimization_barrier((value, blocks[before]))
        blocks[key] = lax.ppermute(value, "recv", perm)
        if 5 <= at < 14 and at % 3 == 2:
            keys = [send[0] for send in STEPS[at // 3 - 1]]
            total = contract(response, place, keys, [blocks[k] for k in keys], total, False)
    for keys in LAST:
        total = contract(response, place, keys, [blocks[k] for k in keys], total, keys is LAST[-1])
    moved = lax.all_to_all(total, "freq", split_axis=0, concat_axis=0, tiled=True)
    moved = moved.reshape(-1, moved.shape[2])
    high, low = make_table()
    start = window_onset.T.reshape(2 * focal, 1)
    end = window_end.T.reshape(2 * focal, 1)
    return transform(moved, jnp.asarray(high), jnp.asarray(low), start, end, focal)


def solution(mesh):
    in_specs = (
        P(None, "freq", "recv", None),
        P(None, "freq", None, "recv"),
        P(None, ("recv", "freq")),
        P(None, ("recv", "freq")),
    )
    out_specs = P(None, ("recv", "freq"), None)
    return jax.shard_map(
        per_device, mesh=mesh, in_specs=in_specs, out_specs=out_specs, check_vma=False
    )
```
